512 devices in a mesh: user: 16 (over x_lo, y, core), item: 32 (over z, x_hi).
Axes of the slice: x: 4 (x_hi: 2, x_lo: 2; x = x_hi * 2 + x_lo), y: 4, z: 16, core: 2. Of those that a mesh axis runs over, the one named last changes fastest.
Arguments:
- user_emb: float32 [24576, 128], P(('user', 'item')), may hold values from -6 to 6
- item_emb: float32 [65536, 128], P(('item', 'user')), may hold values from -6 to 6
- user_deg: int32 [24576], P('user'), may hold values from 1 to 8
- item_deg: int32 [65536], P('item'), may hold values from 1 to 8
- tile_rows: int32 [16, 32, 128], P('user', 'item'), may hold values from 0 to 11
- tile_cols: int32 [16, 32, 128], P('user', 'item'), may hold values from 0 to 15
- tile_count: int32 [16, 32], P('user', 'item'), may hold values from 1 to 128, as said below
- tiles: bfloat16 [16, 32, 128, 128, 128], P('user', 'item'), may hold values from -0.125 to 0.125
Outputs:
- user_out: float32 [24576, 128], P(('user', 'item'))
- item_out: float32 [65536, 128], P(('item', 'user'))
The draws below stay inside these ranges and needn't reach their ends.
Inputs may be any that keep to these rules, and one draw needn't show every extreme that they name: `tile_count`: every device has at least one live slot; on some device all 128 slots are live.
All inputs are finite; a program needn't handle non-finite values.
Results may differ from the reference program's by a relative error of at most 0.0029.
Values may be sent and summed in bfloat16 or wider, within the bound.
A program may use at most 64 MiB of HBM per device.

```python
import jax
import jax.numpy as jnp
from jax import lax

D = 128
BLK = 128
UBD = 12
IBD = 16
TPD = 128
USERS = 24576
ITEMS = 65536
N_USER = 16
N_ITEM = 32


def draw_tile_count(key, part):
    key = jax.random.fold_in(key, 7)
    first_key, second_key, third_key = jax.random.split(key, 3)
    first_draw = jax.random.randint(first_key, (N_USER * N_ITEM,), 1, TPD + 1, dtype=jnp.int32)
    second_draw = jax.random.randint(second_key, (N_USER * N_ITEM,), 1, TPD + 1, dtype=jnp.int32)
    counts = jnp.minimum(first_draw, second_draw)
    full_spot = jax.random.randint(third_key, (), 0, N_USER * N_ITEM, dtype=jnp.int32)
    positions = jnp.arange(N_USER * N_ITEM, dtype=jnp.int32)
    counts = jnp.where(positions == full_spot, jnp.int32(TPD), counts)
    return counts.reshape(N_USER, N_ITEM).astype(jnp.int32)


def with_ends(result, stream_key, least, top_value):
    place = [jax.random.randint(jax.random.fold_in(stream_key, axis), (), 0, length) for axis, length in enumerate(result.shape)]
    main_axis = result.shape.index(max(result.shape))
    beside = place[:main_axis] + [(place[main_axis] + 1) % result.shape[main_axis]] + place[main_axis + 1:]
    return result.at[tuple(place)].set(least).at[tuple(beside)].set(top_value)


def shard_levels(own_key, shape, shards, low, largest):
    loudness = 1.0
    for dim, shards_of in shards:
        draws = jax.random.uniform(jax.random.fold_in(jax.random.fold_in(own_key, 6), dim), (shards_of,), jnp.float32, low / len(shards), largest / len(shards))
        loudness = loudness * jnp.repeat(jnp.exp(draws), shape[dim] // shards_of).reshape((-1,) + (1,) * (len(shape) - 1 - dim))
    return loudness


def centred(key, shape, width, most, shards=(), kind=jnp.bfloat16):
    level = shard_levels(key, shape, shards, -0.22, 0.18) if shards else 1.0
    entries = jax.random.normal(key, shape, jnp.float32) * width * level
    return jnp.minimum(jnp.maximum(entries, -most), most).astype(kind)


def setup_inputs(seed: int = 0) -> dict:
    streams_of = jax.random.split(jax.random.key(seed), 9)
    return {
        "user_emb": centred(streams_of[0], (USERS, D), 1.0, 6.0, ((0, 512),), jnp.float32),
        "item_emb": centred(streams_of[1], (ITEMS, D), 1.0, 6.0, ((0, 512),), jnp.float32),
        "user_deg": with_ends(jax.random.randint(streams_of[2], (USERS,), 1, 9), jax.random.fold_in(streams_of[2], 1), 1, 8).astype(jnp.int32),
        "item_deg": with_ends(jax.random.randint(streams_of[3], (ITEMS,), 1, 9), jax.random.fold_in(streams_of[3], 1), 1, 8).astype(jnp.int32),
        "tile_rows": with_ends(jax.random.randint(streams_of[4], (N_USER, N_ITEM, TPD), 0, UBD), jax.random.fold_in(streams_of[4], 1), 0, UBD - 1).astype(jnp.int32),
        "tile_cols": with_ends(jax.random.randint(streams_of[5], (N_USER, N_ITEM, TPD), 0, IBD), jax.random.fold_in(streams_of[5], 1), 0, IBD - 1).astype(jnp.int32),
        "tile_count": draw_tile_count(jax.random.fold_in(streams_of[8], 71), 0),
        "tiles": centred(streams_of[7], (N_USER, N_ITEM, TPD, BLK, BLK), (6 * TPD * N_ITEM // UBD) ** -0.5, 0.125, ((0, 16), (1, 32))),
    }


def reference(user_emb, item_emb, user_deg, item_deg, tile_rows, tile_cols, tile_count, tiles):
    user_scale = lax.rsqrt(user_deg.astype(jnp.float32))
    item_scale = lax.rsqrt(item_deg.astype(jnp.float32))
    user_src = (user_emb * user_scale[:, None]).astype(jnp.bfloat16)
    item_src = (item_emb * item_scale[:, None]).astype(jnp.bfloat16)
    user_grid = user_src.reshape(N_USER, UBD, BLK, D)
    item_grid = item_src.reshape(N_ITEM, IBD, BLK, D)
    slot_ids = jnp.arange(TPD, dtype=jnp.int32)
    user_ids = jnp.arange(UBD, dtype=jnp.int32)
    item_ids = jnp.arange(IBD, dtype=jnp.int32)

    def visit(state_pair, device_index):
        user_total, item_total = state_pair
        row_block = device_index // N_ITEM
        col_block = device_index % N_ITEM
        row_ids = tile_rows[row_block, col_block]
        col_ids = tile_cols[row_block, col_block]
        alive_mask = (slot_ids < tile_count[row_block, col_block]).astype(jnp.float32)
        weights = tiles[row_block, col_block].astype(jnp.float32)
        chosen_items = item_grid[col_block][col_ids].astype(jnp.float32)
        chosen_users = user_grid[row_block][row_ids].astype(jnp.float32)
        user_terms = jnp.einsum('tij,tjd->tid', weights, chosen_items, precision=lax.Precision.HIGHEST)
        item_terms = jnp.einsum('tji,tjd->tid', weights, chosen_users, precision=lax.Precision.HIGHEST)
        pick_rows = (row_ids[:, None] == user_ids[None, :]).astype(jnp.float32) * alive_mask[:, None]
        pick_cols = (col_ids[:, None] == item_ids[None, :]).astype(jnp.float32) * alive_mask[:, None]
        user_part = jnp.einsum('tu,tid->uid', pick_rows, user_terms, precision=lax.Precision.HIGHEST)
        item_part = jnp.einsum('tc,tid->cid', pick_cols, item_terms, precision=lax.Precision.HIGHEST)
        user_total = user_total.at[row_block].add(user_part)
        item_total = item_total.at[col_block].add(item_part)
        return ((user_total, item_total), None)
    start_pair = (jnp.zeros((N_USER, UBD, BLK, D), jnp.float32), jnp.zeros((N_ITEM, IBD, BLK, D), jnp.float32))
    (user_total, item_total), unused = lax.scan(visit, start_pair, jnp.arange(N_USER * N_ITEM, dtype=jnp.int32))
    user_out = user_total.reshape(USERS, D) * user_scale[:, None]
    item_out = item_total.reshape(ITEMS, D) * item_scale[:, None]
    return (user_out, item_out)
```

```python
import functools

import jax
import jax.numpy as jnp
from jax import lax
from jax.experimental import pallas as pl
from jax.experimental.pallas import tpu as pltpu
from jax.sharding import PartitionSpec as P

MESH = pl.DeviceIdType.MESH
F32, BF16, I32 = jnp.float32, jnp.bfloat16, jnp.int32

USERS_AXIS = 16
BLOCK = 128
SLOTS = 128
UBLOCKS, IBLOCKS = 12, 16
SHARD = 48
UPAIRS = (SLOTS + UBLOCKS) // 2
IPAIRS = (SLOTS + IBLOCKS) // 2
LANES = 256


def iota(shape, dim):
    return lax.broadcasted_iota(I32, shape, dim)


def count(mask, dim):
    return jnp.sum(jnp.where(mask, 1, 0).astype(I32), axis=dim, keepdims=True)


def column(lanes):
    eye = iota((SLOTS, SLOTS), 0) == iota((SLOTS, SLOTS), 1)
    return jnp.sum(jnp.where(eye, lanes, 0), axis=1, keepdims=True)


def order(keys, others, live):
    keys_c, others_c = column(keys), column(others)
    at_lane, at_row = iota((SLOTS, SLOTS), 1), iota((SLOTS, SLOTS), 0)
    alive_l = at_lane < live
    alive_c = iota((SLOTS, 1), 0) < live
    ahead = (keys_c == keys) & (at_lane < at_row) & alive_l
    rank_c = count(ahead, 1)
    hits_l = count((keys_c == at_lane) & (at_row < live), 0)
    hits_c = column(hits_l)
    padded_l = ((hits_l + 1) >> 1) << 1
    padded_c = ((hits_c + 1) >> 1) << 1
    base_l = jnp.sum(jnp.where(at_row < at_lane, padded_c, 0), axis=0, keepdims=True)
    base_c = jnp.sum(jnp.where(at_lane < at_row, padded_l, 0), axis=1, keepdims=True)
    place_c = jnp.sum(jnp.where(at_lane < keys_c, padded_l, 0), axis=1, keepdims=True) + rank_c
    places = iota((SLOTS, LANES), 1)
    slots = iota((SLOTS, LANES), 0)
    mine = (place_c == places) & alive_c
    slot = jnp.sum(jnp.where(mine, slots + 1, 0), axis=0, keepdims=True)
    slot = jnp.where(slot == 0, SLOTS, slot - 1)
    other = jnp.sum(jnp.where(mine, others_c, 0), axis=0, keepdims=True)
    opens = (base_c == places) & (hits_c > 0)
    keep = 1 - jnp.minimum(count(opens, 0), 1)
    last = ((base_l + padded_l) >> 1) - 1
    last = jnp.maximum(last, 0)
    some = jnp.minimum(hits_l, 1)
    return slot, other, keep, last, some


def own_scale(deg_ref, first, rows):
    blocks = deg_ref.shape[0]
    out = jnp.zeros((rows, 1), I32)
    for b in range(blocks):
        here = iota((rows, BLOCK), 1) + b * BLOCK == iota((rows, BLOCK), 0) + first
        out = out + jnp.sum(jnp.where(here, deg_ref[b : b + 1, :], 0), axis=1, keepdims=True)
    return lax.rsqrt(out.astype(F32))


def layer(
    user_emb, item_emb, user_deg, item_deg, rows_ref, cols_ref, live_ref, tiles_hbm,
    user_out, item_out,
    tiles, item_src, users, user_src_t, meta_v, meta, run_u, run_i, part_u, part_i,
    got1, send2, got2, got_i,
    local_sem, ag_i_s, ag_i_r, ag_a_s, ag_a_r, ag_b_s, ag_b_r, rs1_s, rs1_r, rs2_s, rs2_r, rsi_s, rsi_r,
):
    u, i = lax.axis_index("user"), lax.axis_index("item")
    z, xh = i // 2, lax.rem(i, 2)
    zh, zl = z // 4, lax.rem(z, 4)
    kind = 2 * zl + xh

    def at(dz, other):
        half = 1 - xh if other else xh
        return {"item": 2 * lax.rem(z + dz + 16, 16) + half}

    load = pltpu.make_async_copy(tiles_hbm.at[0, 0], tiles.at[pl.ds(0, SLOTS)], local_sem.at[0])
    load.start()

    barrier = pltpu.get_barrier_semaphore()
    for k in range(1, 16):
        pl.semaphore_signal(barrier, inc=1, device_id={"user": lax.rem(u + k, 16)}, device_id_type=MESH)
    near = [(dz, o) for dz in (-2, -1, 0, 1, 2) for o in (False, True) if dz or o]
    far = [(4, False), (8, False), (12, False)]
    for dz, o in near + far:
        pl.semaphore_signal(barrier, inc=1, device_id=at(dz, o), device_id_type=MESH)

    scale_u = own_scale(user_deg, i * SHARD, SHARD)
    scale_i = own_scale(item_deg, u * BLOCK, BLOCK)
    item_src[u] = (item_emb[...] * scale_i).astype(BF16)
    users[zh, kind] = (user_emb[...] * scale_u).astype(BF16)
    pl.semaphore_wait(barrier, 15 + len(near) + len(far))

    ag_a, ag_i = [], []
    for k in range(1, 4):
        ag_a.append(pltpu.make_async_remote_copy(
            src_ref=users.at[zh, kind], dst_ref=users.at[zh, kind], send_sem=ag_a_s.at[k], recv_sem=ag_a_r.at[k],
            device_id=at(4 * k, False), device_id_type=MESH))
    for c in ag_a:
        c.start()
    for k in range(1, 16):
        ag_i.append(pltpu.make_async_remote_copy(
            src_ref=item_src.at[u], dst_ref=item_src.at[u], send_sem=ag_i_s.at[k], recv_sem=ag_i_r.at[k],
            device_id={"user": lax.rem(u + k, 16)}, device_id_type=MESH))
    for c in ag_i:
        c.start()

    rows, cols, live = rows_ref[0], cols_ref[0], live_ref[0, 0]
    parts = order(rows, cols, live) + order(cols, rows, live)
    meta_v[...] = jnp.zeros_like(meta_v)
    for n, part in enumerate(parts):
        meta_v[n : n + 1, 0 : part.shape[1]] = part
    to_scalar = pltpu.make_async_copy(meta_v, meta, local_sem.at[1])
    to_scalar.start()
    tiles[SLOTS] = jnp.zeros((BLOCK, BLOCK), BF16)
    to_scalar.wait()

    for c in ag_a:
        c.wait_recv()
    near_b = [(0, True), (1, False), (1, True), (-1, False), (-1, True)]
    ag_b = []

    def hop2(up):
        return 2 * lax.rem(z + 16 + jnp.where(up, 2, -2), 16)

    for n, (dz, o) in enumerate(near_b):
        ag_b.append(pltpu.make_async_remote_copy(
            src_ref=users.at[:, kind], dst_ref=users.at[:, kind], send_sem=ag_b_s.at[n], recv_sem=ag_b_r.at[n],
            device_id=at(dz, o), device_id_type=MESH))
    for half in range(2):
        ag_b.append(pltpu.make_async_remote_copy(
            src_ref=users.at[:, kind], dst_ref=users.at[:, kind], send_sem=ag_b_s.at[5 + half],
            recv_sem=ag_b_r.at[5 + xh], device_id={"item": hop2(xh == 0) + half}, device_id_type=MESH))
    for c in ag_b:
        c.start()

    load.wait()
    for c in ag_i:
        c.wait_recv()

    def user_step(q, acc):
        s0, s1 = meta[0, 2 * q], meta[0, 2 * q + 1]
        c0, c1 = meta[1, 2 * q], meta[1, 2 * q + 1]
        keep = meta[2, 2 * q].astype(F32)
        left = jnp.concatenate([tiles[s0], tiles[s1]], axis=1)
        right = jnp.concatenate([item_src[c0], item_src[c1]], axis=0)
        acc = acc * keep + jnp.dot(left, right, preferred_element_type=F32)
        run_u[q] = acc
        return acc

    lax.fori_loop(0, UPAIRS, user_step, jnp.zeros((BLOCK, BLOCK), F32), unroll=2)
    for r in range(UBLOCKS):
        total = (run_u[meta[3, r]] * meta[4, r].astype(F32)).astype(BF16)
        for j in range(8):
            g = 8 * r + j
            part_u[g // 24, (g % 24) // 3, 16 * (g % 3) : 16 * (g % 3) + 16, :] = total[16 * j : 16 * j + 16]

    rs1 = []
    for n, (dz, o) in enumerate(near_b):
        half = 1 - xh if o else xh
        there = 2 * lax.rem(zl + dz + 4, 4) + half
        rs1.append(pltpu.make_async_remote_copy(
            src_ref=part_u.at[:, there], dst_ref=got1.at[n], send_sem=rs1_s.at[n], recv_sem=rs1_r.at[n],
            device_id=at(dz, o), device_id_type=MESH))
    for half in range(2):
        there = 2 * lax.rem(zl + 2, 4) + half
        rs1.append(pltpu.make_async_remote_copy(
            src_ref=part_u.at[:, there], dst_ref=got1.at[5 + xh], send_sem=rs1_s.at[5 + half],
            recv_sem=rs1_r.at[5 + xh], device_id={"item": hop2(half == 0) + half}, device_id_type=MESH))
    for c in rs1:
        c.start()

    for n in range(5):
        ag_b[n].wait_recv()
    for half in range(2):
        pltpu.make_async_remote_copy(
            src_ref=users.at[:, kind], dst_ref=users.at[:, 2 * lax.rem(zl + 2, 4) + half], send_sem=ag_b_s.at[5 + half],
            recv_sem=ag_b_r.at[5 + half], device_id=at(1, False), device_id_type=MESH).wait_recv()
    for r in range(UBLOCKS):
        groups = []
        for j in range(8):
            g = 8 * r + j
            groups.append(users[g // 24, (g % 24) // 3, 16 * (g % 3) : 16 * (g % 3) + 16, :])
        user_src_t[r] = jnp.concatenate(groups, axis=0).T

    def item_step(q, acc):
        s0, s1 = meta[5, 2 * q], meta[5, 2 * q + 1]
        r0, r1 = meta[6, 2 * q], meta[6, 2 * q + 1]
        keep = meta[7, 2 * q].astype(F32)
        left = jnp.concatenate([user_src_t[r0], user_src_t[r1]], axis=1)
        right = jnp.concatenate([tiles[s0], tiles[s1]], axis=0)
        acc = acc * keep + jnp.dot(left, right, preferred_element_type=F32)
        run_i[q] = acc
        return acc

    lax.fori_loop(0, IPAIRS, item_step, jnp.zeros((BLOCK, BLOCK), F32), unroll=2)
    for c in range(IBLOCKS):
        part_i[c] = (run_i[meta[8, c]] * meta[9, c].astype(F32)).astype(BF16)
    rsi = []
    for k in range(1, 16):
        there = lax.rem(u + k, 16)
        rsi.append(pltpu.make_async_remote_copy(
            src_ref=part_i.at[there], dst_ref=got_i.at[k], send_sem=rsi_s.at[k], recv_sem=rsi_r.at[k],
            device_id={"user": there}, device_id_type=MESH))
    for c in rsi:
        c.start()

    for n in range(5):
        rs1[n].wait_recv()
    for half in range(2):
        pltpu.make_async_remote_copy(
            src_ref=part_u.at[:, kind], dst_ref=got1.at[5 + half], send_sem=rs1_s.at[5 + half],
            recv_sem=rs1_r.at[5 + half], device_id=at(1, False), device_id_type=MESH).wait_recv()
    for h in range(4):
        total = part_u[h, kind].astype(F32)
        for n in range(7):
            total = total + got1[n, h].astype(F32)
        send2[h] = total
        got2[0, h] = total.astype(BF16)
    rs2 = []
    for k in range(1, 4):
        there = lax.rem(zh + k, 4)
        rs2.append(pltpu.make_async_remote_copy(
            src_ref=got2.at[0, there], dst_ref=got2.at[k, 0], send_sem=rs2_s.at[k], recv_sem=rs2_r.at[k],
            device_id=at(4 * k, False), device_id_type=MESH))
    for c in rs2:
        c.start()

    for c in rsi:
        c.wait_recv()
    total = part_i[u].astype(F32)
    for k in range(1, 16):
        total = total + got_i[k].astype(F32)
    item_out[...] = total.T * scale_i

    for c in rs2:
        c.wait_recv()
    total = send2[zh]
    for k in range(1, 4):
        total = total + got2[k, 0].astype(F32)
    user_out[...] = total * scale_u

    for c in ag_a + ag_i + ag_b + rs1 + rs2 + rsi:
        c.wait_send()


def keep_both(a, b, c, d):
    c[...] = a[...]
    d[...] = b[...]


def local(user_emb, item_emb, user_deg, item_deg, tile_rows, tile_cols, tile_count, tiles):
    vmem = pl.BlockSpec(memory_space=pltpu.VMEM)
    smem = pl.BlockSpec(memory_space=pltpu.SMEM)
    dma = pltpu.SemaphoreType.DMA
    outs = (
        jax.ShapeDtypeStruct((SHARD, BLOCK), F32),
        jax.ShapeDtypeStruct((BLOCK, BLOCK), F32),
    )
    half_done = pl.pallas_call(
        layer,
        out_shape=outs,
        in_specs=[vmem] * 6 + [smem, pl.BlockSpec(memory_space=pl.ANY)],
        out_specs=(vmem, vmem),
        scratch_shapes=[
            pltpu.VMEM((SLOTS + 1, BLOCK, BLOCK), BF16),
            pltpu.VMEM((IBLOCKS, BLOCK, BLOCK), BF16),
            pltpu.VMEM((4, 8, SHARD, BLOCK), BF16),
            pltpu.VMEM((UBLOCKS, BLOCK, BLOCK), BF16),
            pltpu.VMEM((16, LANES), I32),
            pltpu.SMEM((16, LANES), I32),
            pltpu.VMEM((UPAIRS, BLOCK, BLOCK), F32),
            pltpu.VMEM((IPAIRS, BLOCK, BLOCK), F32),
            pltpu.VMEM((4, 8, SHARD, BLOCK), BF16),
            pltpu.VMEM((IBLOCKS, BLOCK, BLOCK), BF16),
            pltpu.VMEM((7, 4, SHARD, BLOCK), BF16),
            pltpu.VMEM((4, SHARD, BLOCK), F32),
            pltpu.VMEM((4, 4, SHARD, BLOCK), BF16),
            pltpu.VMEM((16, BLOCK, BLOCK), BF16),
            dma((2,)),
            dma((16,)), dma((16,)),
            dma((4,)), dma((4,)),
            dma((7,)), dma((7,)),
            dma((7,)), dma((7,)),
            dma((4,)), dma((4,)),
            dma((16,)), dma((16,)),
        ],
        compiler_params=pltpu.CompilerParams(
            collective_id=0, has_side_effects=True, vmem_limit_bytes=40 * 1024 * 1024
        ),
        name="layer",
    )(
        user_emb, item_emb, user_deg.reshape(UBLOCKS, BLOCK), item_deg.reshape(IBLOCKS, BLOCK),
        tile_rows, tile_cols, tile_count, tiles,
    )
    return pl.pallas_call(
        keep_both, out_shape=outs, in_specs=[vmem, vmem], out_specs=(vmem, vmem), name="keep"
    )(*half_done)


def solution(mesh):
    return jax.shard_map(
        local,
        mesh=mesh,
        in_specs=(
            P(("user", "item"), None),
            P(("item", "user"), None),
            P("user"),
            P("item"),
            P("user", "item", None),
            P("user", "item", None),
            P("user", "item"),
            P("user", "item", None, None, None),
        ),
        out_specs=(P(("user", "item"), None), P(("item", "user"), None)),
        check_vma=False,
    )
```

```python
import functools

import jax
import jax.numpy as jnp
from jax import lax
from jax.experimental import pallas as pl
from jax.experimental.pallas import tpu as pltpu
from jax.sharding import PartitionSpec as P

MESH = pl.DeviceIdType.MESH
F32, BF16, I32 = jnp.float32, jnp.bfloat16, jnp.int32

USERS_AXIS = 16
BLOCK = 128
SLOTS = 128
UBLOCKS, IBLOCKS = 12, 16
SHARD = 48
UPAIRS = (SLOTS + UBLOCKS) // 2
IPAIRS = (SLOTS + IBLOCKS) // 2
LANES = 256
UUNROLL, IUNROLL = 35, 24


def iota(shape, dim):
    return lax.broadcasted_iota(I32, shape, dim)


def count(mask, dim):
    return jnp.sum(jnp.where(mask, 1, 0).astype(I32), axis=dim, keepdims=True)


def column(lanes):
    eye = iota((SLOTS, SLOTS), 0) == iota((SLOTS, SLOTS), 1)
    return jnp.sum(jnp.where(eye, lanes, 0), axis=1, keepdims=True)


def order(keys, others, live):
    keys_c, others_c = column(keys), column(others)
    at_lane, at_row = iota((SLOTS, SLOTS), 1), iota((SLOTS, SLOTS), 0)
    alive_l = at_lane < live
    alive_c = iota((SLOTS, 1), 0) < live
    ahead = (keys_c == keys) & (at_lane < at_row) & alive_l
    rank_c = count(ahead, 1)
    hits_l = count((keys_c == at_lane) & (at_row < live), 0)
    hits_c = column(hits_l)
    padded_l = ((hits_l + 1) >> 1) << 1
    padded_c = ((hits_c + 1) >> 1) << 1
    base_l = jnp.sum(jnp.where(at_row < at_lane, padded_c, 0), axis=0, keepdims=True)
    base_c = jnp.sum(jnp.where(at_lane < at_row, padded_l, 0), axis=1, keepdims=True)
    place_c = jnp.sum(jnp.where(at_lane < keys_c, padded_l, 0), axis=1, keepdims=True) + rank_c
    places = iota((SLOTS, LANES), 1)
    slots = iota((SLOTS, LANES), 0)
    mine = (place_c == places) & alive_c
    slot = jnp.sum(jnp.where(mine, slots + 1, 0), axis=0, keepdims=True)
    slot = jnp.where(slot == 0, SLOTS, slot - 1)
    other = jnp.sum(jnp.where(mine, others_c, 0), axis=0, keepdims=True)
    opens = (base_c == places) & (hits_c > 0)
    keep = 1 - jnp.minimum(count(opens, 0), 1)
    last = ((base_l + padded_l) >> 1) - 1
    last = jnp.maximum(last, 0)
    some = jnp.minimum(hits_l, 1)
    return slot, other, keep, last, some


def own_scale(deg_ref, first, rows):
    blocks = deg_ref.shape[0]
    out = jnp.zeros((rows, 1), I32)
    for b in range(blocks):
        here = iota((rows, BLOCK), 1) + b * BLOCK == iota((rows, BLOCK), 0) + first
        out = out + jnp.sum(jnp.where(here, deg_ref[b : b + 1, :], 0), axis=1, keepdims=True)
    return lax.rsqrt(out.astype(F32))


def layer(
    user_emb_h, item_emb_h, user_deg_h, item_deg_h, rows_h, cols_h, live_h, tiles_h,
    user_out, item_out,
    user_emb, item_emb, user_deg, item_deg, rows_v, cols_v, live_v,
    tiles, item_src, users, user_src_t, meta_v, meta, run_u, run_i, part_u, part_i,
    got1, keep1, send2, got2, got_i,
    local_sem, ag_a_s, ag_a_r, ag_b_s, ag_b_r, ag_i_s, ag_i_r, ag_f_s, ag_f_r,
    rs1_s, rs1_r, rs2_s, rs2_r, rsi_s, rsi_r,
):
    u, i = lax.axis_index("user"), lax.axis_index("item")
    z, xh = i // 2, lax.rem(i, 2)
    zh, zl = z // 4, lax.rem(z, 4)
    kind = 2 * zl + xh
    twin = u + 1 - 2 * lax.rem(u, 2)

    def plane(dz):
        return lax.rem(z + dz + 16, 16)

    def at(dz, other):
        return {"item": 2 * plane(dz) + (1 - xh if other else xh)}

    def send(src, dst, sems, where, there):
        return pltpu.make_async_remote_copy(
            src_ref=src, dst_ref=dst, send_sem=sems[0].at[where[0]], recv_sem=sems[1].at[where[1]],
            device_id=there, device_id_type=MESH)

    ins = [
        pltpu.make_async_copy(a, b, local_sem.at[n]) for n, (a, b) in enumerate((
            (item_deg_h, item_deg), (item_emb_h, item_emb), (user_deg_h, user_deg), (user_emb_h, user_emb),
            (rows_h, rows_v), (cols_h, cols_v), (live_h, live_v), (tiles_h.at[0, 0], tiles.at[pl.ds(0, SLOTS)])))
    ]
    for c in ins:
        c.start()

    barrier = pltpu.get_barrier_semaphore()
    near = [(dz, o) for dz in (-2, -1, 0, 1, 2) for o in (False, True) if dz or o]
    far = [(8, False), (4, False), (12, False)]
    for dz, o in far + near:
        pl.semaphore_signal(barrier, inc=1, device_id=at(dz, o), device_id_type=MESH)
    for k in range(1, 8):
        pl.semaphore_signal(barrier, inc=1, device_id={"user": lax.rem(u + 2 * k, 16)}, device_id_type=MESH)
    pl.semaphore_signal(barrier, inc=1, device_id={"user": twin}, device_id_type=MESH)
    for k in range(1, 8):
        pl.semaphore_signal(barrier, inc=1, device_id={"user": lax.rem(twin + 2 * k, 16)}, device_id_type=MESH)

    for n in range(4):
        ins[n].wait()
    scale_i = own_scale(item_deg, u * BLOCK, BLOCK)
    item_src[u] = (item_emb[...] * scale_i).astype(BF16)
    scale_u = own_scale(user_deg, i * SHARD, SHARD)
    users[zh, kind] = (user_emb[...] * scale_u).astype(BF16)
    pl.semaphore_wait(barrier, 15 + len(near) + len(far))

    ag_a = [
        send(users.at[zh, kind], users.at[zh, kind], (ag_a_s, ag_a_r), (k, k), at(4 * k, False)) for k in (2, 1, 3)
    ]
    for c in ag_a:
        c.start()
    ag_i = [
        send(item_src.at[u], item_src.at[u], (ag_i_s, ag_i_r), (k, k), {"user": lax.rem(u + 2 * k, 16)})
        for k in range(1, 8)
    ]
    for c in ag_i:
        c.start()
    ag_f = [send(item_src.at[u], item_src.at[u], (ag_f_s, ag_f_r), (0, 0), {"user": twin})]
    ag_f[0].start()

    turn = 2 * plane(2) * (1 - xh) + 2 * plane(-2) * xh
    ag_b = []

    def spread(h):
        row = users.at[h, kind]
        for dz, o in ((0, True), (1, False), (1, True), (-1, False), (-1, True)):
            ag_b.append(send(row, row, (ag_b_s, ag_b_r), (0, 0), at(dz, o)))
        for half in range(2):
            ag_b.append(send(row, row, (ag_b_s, ag_b_r), (0, 0), {"item": turn + half}))
        for c in ag_b[-7:]:
            c.start()

    spread(zh)

    for n in range(4, 7):
        ins[n].wait()
    rows, cols, live = rows_v[0], cols_v[0], live_v[...]
    parts = order(rows, cols, live) + order(cols, rows, live)
    meta_v[...] = jnp.zeros_like(meta_v)
    for n, part in enumerate(parts):
        meta_v[n : n + 1, 0 : part.shape[1]] = part
    to_scalar = pltpu.make_async_copy(meta_v, meta, local_sem.at[8])
    to_scalar.start()
    tiles[SLOTS] = jnp.zeros((BLOCK, BLOCK), BF16)

    for k in range(1, 8):
        ag_i[k - 1].wait_recv()
        came = lax.rem(u - 2 * k + 16, 16)
        c = send(item_src.at[came], item_src.at[came], (ag_f_s, ag_f_r), (0, 0), {"user": twin})
        c.start()
        ag_f.append(c)
    for n, k in ((1, 1), (2, 3), (0, 2)):
        ag_a[n].wait_recv()
        spread(lax.rem(zh - k + 4, 4))

    to_scalar.wait()
    ins[7].wait()
    send(item_src.at[0:8], item_src.at[0:8], (ag_f_s, ag_f_r), (0, 0), {"user": twin}).wait_recv()

    def user_step(q, acc):
        s0, s1 = meta[0, 2 * q], meta[0, 2 * q + 1]
        c0, c1 = meta[1, 2 * q], meta[1, 2 * q + 1]
        keep = meta[2, 2 * q].astype(F32)
        left = jnp.concatenate([tiles[s0], tiles[s1]], axis=1)
        right = jnp.concatenate([item_src[c0], item_src[c1]], axis=0)
        acc = acc * keep + jnp.dot(left, right, preferred_element_type=F32)
        run_u[q] = acc
        return acc

    lax.fori_loop(0, UPAIRS, user_step, jnp.zeros((BLOCK, BLOCK), F32), unroll=UUNROLL)
    for r in range(UBLOCKS):
        total = (run_u[meta[3, r]] * meta[4, r].astype(F32)).astype(BF16)
        for j in range(8):
            g = 8 * r + j
            part_u[g // 24, (g % 24) // 3, 16 * (g % 3) : 16 * (g % 3) + 16, :] = total[16 * j : 16 * j + 16]

    rs1 = []
    for k in (2, 1, 3, 0):
        for n, (dz, o) in enumerate(((0, True), (1, False), (1, True), (-1, False), (-1, True))):
            there = 2 * lax.rem(zl + dz + 4, 4) + (1 - xh if o else xh)
            rs1.append(send(part_u.at[lax.rem(plane(dz) // 4 + k, 4), there], got1.at[k, n], (rs1_s, rs1_r), (0, k), at(dz, o)))
        for half in range(2):
            there = 2 * lax.rem(zl + 2, 4) + half
            dz = 2 - 4 * half
            rs1.append(send(part_u.at[lax.rem(plane(dz) // 4 + k, 4), there], got1.at[k, 5 + xh], (rs1_s, rs1_r), (0, k),
                            {"item": 2 * plane(dz) + half}))
        for c in rs1[-7:]:
            c.start()

    send(users.at[:, 0:7], users.at[:, 0:7], (ag_b_s, ag_b_r), (0, 0), at(1, False)).wait_recv()
    for r in range(UBLOCKS):
        groups = []
        for j in range(8):
            g = 8 * r + j
            groups.append(users[g // 24, (g % 24) // 3, 16 * (g % 3) : 16 * (g % 3) + 16, :])
        user_src_t[r] = jnp.concatenate(groups, axis=0).T

    def item_step(q, acc):
        s0, s1 = meta[5, 2 * q], meta[5, 2 * q + 1]
        r0, r1 = meta[6, 2 * q], meta[6, 2 * q + 1]
        keep = meta[7, 2 * q].astype(F32)
        left = jnp.concatenate([user_src_t[r0], user_src_t[r1]], axis=1)
        right = jnp.concatenate([tiles[s0], tiles[s1]], axis=0)
        acc = acc * keep + jnp.dot(left, right, preferred_element_type=F32)
        run_i[q] = acc
        return acc

    lax.fori_loop(0, IPAIRS, item_step, jnp.zeros((BLOCK, BLOCK), F32), unroll=IUNROLL)
    for c in range(IBLOCKS):
        part_i[c] = (run_i[meta[8, c]] * meta[9, c].astype(F32)).astype(BF16)
    rsi = []
    for k in range(1, 16):
        there = lax.rem(u + k, 16)
        rsi.append(send(part_i.at[there], got_i.at[k], (rsi_s, rsi_r), (0, 0), {"user": there}))
    for c in rsi:
        c.start()

    rs2 = []
    for k in (2, 1, 3, 0):
        send(got1.at[k], got1.at[k], (rs1_s, rs1_r), (0, k), at(1, False)).wait_recv()
        total = part_u[lax.rem(zh + k, 4), kind].astype(F32)
        for n in range(7):
            total = total + got1[k, n].astype(F32)
        if k:
            send2[k] = total.astype(BF16)
            rs2.append(send(send2.at[k], got2.at[k], (rs2_s, rs2_r), (0, 0), at(4 * k, False)))
            rs2[-1].start()
        else:
            keep1[...] = total

    send(got_i.at[1:16], got_i.at[1:16], (rsi_s, rsi_r), (0, 0), {"user": twin}).wait_recv()
    total = part_i[u].astype(F32)
    for k in range(1, 16):
        total = total + got_i[k].astype(F32)
    item_out[...] = total.T * scale_i

    send(got2.at[1:4], got2.at[1:4], (rs2_s, rs2_r), (0, 0), at(1, False)).wait_recv()
    total = keep1[...]
    for k in range(1, 4):
        total = total + got2[k].astype(F32)
    user_out[...] = total * scale_u

    for c in ag_a + ag_i:
        c.wait_send()
    send(item_src.at[0:8], item_src.at[0:8], (ag_f_s, ag_f_r), (0, 0), {"user": twin}).wait_send()
    send(users.at[:, 0:7], users.at[:, 0:7], (ag_b_s, ag_b_r), (0, 0), at(1, False)).wait_send()
    send(part_u.at[:, 0:7], part_u.at[:, 0:7], (rs1_s, rs1_r), (0, 0), at(1, False)).wait_send()
    send(got_i.at[1:16], got_i.at[1:16], (rsi_s, rsi_r), (0, 0), {"user": twin}).wait_send()
    send(got2.at[1:4], got2.at[1:4], (rs2_s, rs2_r), (0, 0), at(1, False)).wait_send()


def hand_over(a, b, c, d, sem):
    copies = [pltpu.make_async_copy(a, c, sem.at[0]), pltpu.make_async_copy(b, d, sem.at[1])]
    for copy in copies:
        copy.start()
    for copy in copies:
        copy.wait()


def local(user_emb, item_emb, user_deg, item_deg, tile_rows, tile_cols, tile_count, tiles):
    hbm = pl.BlockSpec(memory_space=pltpu.HBM)
    dma = pltpu.SemaphoreType.DMA
    outs = (jax.ShapeDtypeStruct((SHARD, BLOCK), F32), jax.ShapeDtypeStruct((BLOCK, BLOCK), F32))
    vmem = pl.BlockSpec(memory_space=pltpu.VMEM)
    sums = pl.pallas_call(
        layer,
        out_shape=(pltpu.VMEM((SHARD, BLOCK), F32), pltpu.VMEM((BLOCK, BLOCK), F32)),
        in_specs=[hbm] * 8,
        out_specs=(vmem, vmem),
        scratch_shapes=[
            pltpu.VMEM((SHARD, BLOCK), F32),
            pltpu.VMEM((BLOCK, BLOCK), F32),
            pltpu.VMEM((UBLOCKS, BLOCK), I32),
            pltpu.VMEM((IBLOCKS, BLOCK), I32),
            pltpu.VMEM((1, 1, SLOTS), I32),
            pltpu.VMEM((1, 1, SLOTS), I32),
            pltpu.VMEM((1, 1), I32),
            pltpu.VMEM((SLOTS + 1, BLOCK, BLOCK), BF16),
            pltpu.VMEM((IBLOCKS, BLOCK, BLOCK), BF16),
            pltpu.VMEM((4, 8, SHARD, BLOCK), BF16),
            pltpu.VMEM((UBLOCKS, BLOCK, BLOCK), BF16),
            pltpu.VMEM((16, LANES), I32),
            pltpu.SMEM((16, LANES), I32),
            pltpu.VMEM((UPAIRS, BLOCK, BLOCK), F32),
            pltpu.VMEM((IPAIRS, BLOCK, BLOCK), F32),
            pltpu.VMEM((4, 8, SHARD, BLOCK), BF16),
            pltpu.VMEM((IBLOCKS, BLOCK, BLOCK), BF16),
            pltpu.VMEM((4, 7, SHARD, BLOCK), BF16),
            pltpu.VMEM((SHARD, BLOCK), F32),
            pltpu.VMEM((4, SHARD, BLOCK), BF16),
            pltpu.VMEM((4, SHARD, BLOCK), BF16),
            pltpu.VMEM((16, BLOCK, BLOCK), BF16),
            dma((11,)),
            dma((4,)), dma((4,)),
            dma((1,)), dma((1,)),
            dma((8,)), dma((8,)),
            dma((1,)), dma((1,)),
            dma((1,)), dma((4,)),
            dma((1,)), dma((1,)),
            dma((1,)), dma((1,)),
        ],
        compiler_params=pltpu.CompilerParams(
            collective_id=0, has_side_effects=True, vmem_limit_bytes=60 * 1024 * 1024
        ),
        name="layer",
    )(
        user_emb, item_emb, user_deg.reshape(UBLOCKS, BLOCK), item_deg.reshape(IBLOCKS, BLOCK),
        tile_rows, tile_cols, tile_count, tiles,
    )
    return pl.pallas_call(
        hand_over,
        out_shape=outs,
        in_specs=[vmem, vmem],
        out_specs=(hbm, hbm),
        scratch_shapes=[dma((2,))],
        compiler_params=pltpu.CompilerParams(vmem_limit_bytes=16 * 1024 * 1024),
        name="hand_over",
    )(*sums)


def solution(mesh):
    return jax.shard_map(
        local,
        mesh=mesh,
        in_specs=(
            P(("user", "item"), None),
            P(("item", "user"), None),
            P("user"),
            P("item"),
            P("user", "item", None),
            P("user", "item", None),
            P("user", "item"),
            P("user", "item", None, None, None),
        ),
        out_specs=(P(("user", "item"), None), P(("item", "user"), None)),
        check_vma=False,
    )
```

```python
import functools

import jax
import jax.numpy as jnp
from jax import lax
from jax.experimental import pallas as pl
from jax.experimental.pallas import tpu as pltpu
from jax.sharding import PartitionSpec as P

MESH = pl.DeviceIdType.MESH
F32, BF16, I32 = jnp.float32, jnp.bfloat16, jnp.int32

USERS_AXIS = 16
BLOCK = 128
SLOTS = 128
UBLOCKS, IBLOCKS = 12, 16
SHARD = 48
UPAIRS = (SLOTS + UBLOCKS) // 2
IPAIRS = (SLOTS + IBLOCKS) // 2
LANES = 256
UUNROLL, IUNROLL = 70, 72


def iota(shape, dim):
    return lax.broadcasted_iota(I32, shape, dim)


def count(mask, dim):
    return jnp.sum(jnp.where(mask, 1, 0).astype(I32), axis=dim, keepdims=True)


def column(lanes):
    eye = iota((SLOTS, SLOTS), 0) == iota((SLOTS, SLOTS), 1)
    return jnp.sum(jnp.where(eye, lanes, 0), axis=1, keepdims=True)


def order(keys, others, live):
    keys_c, others_c = column(keys), column(others)
    at_lane, at_row = iota((SLOTS, SLOTS), 1), iota((SLOTS, SLOTS), 0)
    alive_l = at_lane < live
    alive_c = iota((SLOTS, 1), 0) < live
    ahead = (keys_c == keys) & (at_lane < at_row) & alive_l
    rank_c = count(ahead, 1)
    hits_l = count((keys_c == at_lane) & (at_row < live), 0)
    hits_c = column(hits_l)
    padded_l = ((hits_l + 1) >> 1) << 1
    padded_c = ((hits_c + 1) >> 1) << 1
    base_l = jnp.sum(jnp.where(at_row < at_lane, padded_c, 0), axis=0, keepdims=True)
    base_c = jnp.sum(jnp.where(at_lane < at_row, padded_l, 0), axis=1, keepdims=True)
    place_c = jnp.sum(jnp.where(at_lane < keys_c, padded_l, 0), axis=1, keepdims=True) + rank_c
    places = iota((SLOTS, LANES), 1)
    slots = iota((SLOTS, LANES), 0)
    mine = (place_c == places) & alive_c
    slot = jnp.sum(jnp.where(mine, slots + 1, 0), axis=0, keepdims=True)
    slot = jnp.where(slot == 0, SLOTS, slot - 1)
    other = jnp.sum(jnp.where(mine, others_c, 0), axis=0, keepdims=True)
    opens = (base_c == places) & (hits_c > 0)
    keep = 1 - jnp.minimum(count(opens, 0), 1)
    last = ((base_l + padded_l) >> 1) - 1
    last = jnp.maximum(last, 0)
    some = jnp.minimum(hits_l, 1)
    return slot, other, keep, last, some


def own_scale(deg_ref, first, rows):
    blocks = deg_ref.shape[0]
    out = jnp.zeros((rows, 1), I32)
    for b in range(blocks):
        here = iota((rows, BLOCK), 1) + b * BLOCK == iota((rows, BLOCK), 0) + first
        out = out + jnp.sum(jnp.where(here, deg_ref[b : b + 1, :], 0), axis=1, keepdims=True)
    return lax.rsqrt(out.astype(F32))


def layer(
    user_emb_h, item_emb_h, user_deg_h, item_deg_h, rows_h, cols_h, live_h, tiles_h,
    user_out, item_out,
    user_emb, item_emb, user_deg, item_deg, rows_v, cols_v, live_v,
    tiles, item_src, users, user_src_t, meta_v, meta, run_u, run_i, part_u, part_i,
    got1, keep1, send2, got2, got_i,
    local_sem, ag_a_s, ag_a_r, ag_b_s, ag_b_r, ag_i_s, ag_i_r, ag_f_s, ag_f_r,
    rs1_s, rs1_r, rs2_s, rs2_r, rsi_s, rsi_r,
):
    u, i = lax.axis_index("user"), lax.axis_index("item")
    z, xh = i // 2, lax.rem(i, 2)
    zh, zl = z // 4, lax.rem(z, 4)
    kind = 2 * zl + xh
    twin = u + 1 - 2 * lax.rem(u, 2)

    def plane(dz):
        return lax.rem(z + dz + 16, 16)

    def at(dz, other):
        return {"item": 2 * plane(dz) + (1 - xh if other else xh)}

    def send(src, dst, sems, where, there):
        return pltpu.make_async_remote_copy(
            src_ref=src, dst_ref=dst, send_sem=sems[0].at[where[0]], recv_sem=sems[1].at[where[1]],
            device_id=there, device_id_type=MESH)

    ins = [
        pltpu.make_async_copy(a, b, local_sem.at[n]) for n, (a, b) in enumerate((
            (item_deg_h, item_deg), (item_emb_h, item_emb), (user_deg_h, user_deg), (user_emb_h, user_emb),
            (rows_h, rows_v), (cols_h, cols_v), (live_h, live_v), (tiles_h.at[0, 0], tiles.at[pl.ds(0, SLOTS)])))
    ]
    for c in ins:
        c.start()

    barrier = pltpu.get_barrier_semaphore()
    near = [(dz, o) for dz in (-2, -1, 0, 1, 2) for o in (False, True) if dz or o]
    far = [(8, False), (4, False), (12, False)]
    for dz, o in far + near:
        pl.semaphore_signal(barrier, inc=1, device_id=at(dz, o), device_id_type=MESH)
    for k in range(1, 8):
        pl.semaphore_signal(barrier, inc=1, device_id={"user": lax.rem(u + 2 * k, 16)}, device_id_type=MESH)
    pl.semaphore_signal(barrier, inc=1, device_id={"user": twin}, device_id_type=MESH)
    for k in range(1, 8):
        pl.semaphore_signal(barrier, inc=1, device_id={"user": lax.rem(twin + 2 * k, 16)}, device_id_type=MESH)

    for n in range(4):
        ins[n].wait()
    scale_i = own_scale(item_deg, u * BLOCK, BLOCK)
    item_src[u] = (item_emb[...] * scale_i).astype(BF16)
    scale_u = own_scale(user_deg, i * SHARD, SHARD)
    users[zh, kind] = (user_emb[...] * scale_u).astype(BF16)
    pl.semaphore_wait(barrier, 15 + len(near) + len(far))

    ag_a = [
        send(users.at[zh, kind], users.at[zh, kind], (ag_a_s, ag_a_r), (k, k), at(4 * k, False)) for k in (2, 1, 3)
    ]
    for c in ag_a:
        c.start()
    ag_i = [
        send(item_src.at[u], item_src.at[u], (ag_i_s, ag_i_r), (k, k), {"user": lax.rem(u + 2 * k, 16)})
        for k in range(1, 8)
    ]
    for c in ag_i:
        c.start()
    ag_f = [send(item_src.at[u], item_src.at[u], (ag_f_s, ag_f_r), (0, 0), {"user": twin})]
    ag_f[0].start()

    turn = 2 * plane(2) * (1 - xh) + 2 * plane(-2) * xh
    ag_b = []

    def spread(h):
        row = users.at[h, kind]
        for dz, o in ((0, True), (1, False), (1, True), (-1, False), (-1, True)):
            ag_b.append(send(row, row, (ag_b_s, ag_b_r), (0, 0), at(dz, o)))
        for half in range(2):
            ag_b.append(send(row, row, (ag_b_s, ag_b_r), (0, 0), {"item": turn + half}))
        for c in ag_b[-7:]:
            c.start()


    for n in range(4, 7):
        ins[n].wait()
    rows, cols, live = rows_v[0], cols_v[0], live_v[...]
    parts = order(rows, cols, live) + order(cols, rows, live)
    meta_v[...] = jnp.zeros_like(meta_v)
    for n, part in enumerate(parts):
        meta_v[n : n + 1, 0 : part.shape[1]] = part
    to_scalar = pltpu.make_async_copy(meta_v, meta, local_sem.at[8])
    to_scalar.start()
    tiles[SLOTS] = jnp.zeros((BLOCK, BLOCK), BF16)

    spread(zh)

    for k in range(1, 8):
        ag_i[k - 1].wait_recv()
        came = lax.rem(u - 2 * k + 16, 16)
        c = send(item_src.at[came], item_src.at[came], (ag_f_s, ag_f_r), (0, 0), {"user": twin})
        c.start()
        ag_f.append(c)
    for n, k in ((1, 1), (2, 3), (0, 2)):
        ag_a[n].wait_recv()
        spread(lax.rem(zh - k + 4, 4))

    to_scalar.wait()
    ins[7].wait()
    send(item_src.at[0:8], item_src.at[0:8], (ag_f_s, ag_f_r), (0, 0), {"user": twin}).wait_recv()

    def user_step(q, acc):
        s0, s1 = meta[0, 2 * q], meta[0, 2 * q + 1]
        c0, c1 = meta[1, 2 * q], meta[1, 2 * q + 1]
        keep = meta[2, 2 * q].astype(F32)
        left = jnp.concatenate([tiles[s0], tiles[s1]], axis=1)
        right = jnp.concatenate([item_src[c0], item_src[c1]], axis=0)
        acc = acc * keep + jnp.dot(left, right, preferred_element_type=F32)
        run_u[q] = acc
        return acc

    lax.fori_loop(0, UPAIRS, user_step, jnp.zeros((BLOCK, BLOCK), F32), unroll=UUNROLL)
    for r in range(UBLOCKS):
        total = (run_u[meta[3, r]] * meta[4, r].astype(F32)).astype(BF16)
        for j in range(8):
            g = 8 * r + j
            part_u[g // 24, (g % 24) // 3, 16 * (g % 3) : 16 * (g % 3) + 16, :] = total[16 * j : 16 * j + 16]

    rs1 = []
    for k in (2, 1, 3, 0):
        for n, (dz, o) in enumerate(((0, True), (1, False), (1, True), (-1, False), (-1, True))):
            there = 2 * lax.rem(zl + dz + 4, 4) + (1 - xh if o else xh)
            rs1.append(send(part_u.at[lax.rem(plane(dz) // 4 + k, 4), there], got1.at[k, n], (rs1_s, rs1_r), (0, k), at(dz, o)))
        for half in range(2):
            there = 2 * lax.rem(zl + 2, 4) + half
            dz = 2 - 4 * half
            rs1.append(send(part_u.at[lax.rem(plane(dz) // 4 + k, 4), there], got1.at[k, 5 + xh], (rs1_s, rs1_r), (0, k),
                            {"item": 2 * plane(dz) + half}))
        for c in rs1[-7:]:
            c.start()

    send(users.at[:, 0:7], users.at[:, 0:7], (ag_b_s, ag_b_r), (0, 0), at(1, False)).wait_recv()
    for r in range(UBLOCKS):
        groups = []
        for j in range(8):
            g = 8 * r + j
            groups.append(users[g // 24, (g % 24) // 3, 16 * (g % 3) : 16 * (g % 3) + 16, :])
        user_src_t[r] = jnp.concatenate(groups, axis=0).T

    def item_step(q, acc):
        s0, s1 = meta[5, 2 * q], meta[5, 2 * q + 1]
        r0, r1 = meta[6, 2 * q], meta[6, 2 * q + 1]
        keep = meta[7, 2 * q].astype(F32)
        left = jnp.concatenate([user_src_t[r0], user_src_t[r1]], axis=1)
        right = jnp.concatenate([tiles[s0], tiles[s1]], axis=0)
        acc = acc * keep + jnp.dot(left, right, preferred_element_type=F32)
        run_i[q] = acc
        return acc

    lax.fori_loop(0, IPAIRS, item_step, jnp.zeros((BLOCK, BLOCK), F32), unroll=IUNROLL)
    for c in range(IBLOCKS):
        part_i[c] = (run_i[meta[8, c]] * meta[9, c].astype(F32)).astype(BF16)
    rsi = []
    for k in range(1, 16):
        there = lax.rem(u + k, 16)
        rsi.append(send(part_i.at[there], got_i.at[k], (rsi_s, rsi_r), (0, 0), {"user": there}))
    for c in rsi:
        c.start()

    rs2 = []
    for k in (2, 1, 3, 0):
        send(got1.at[k], got1.at[k], (rs1_s, rs1_r), (0, k), at(1, False)).wait_recv()
        total = part_u[lax.rem(zh + k, 4), kind].astype(F32)
        for n in range(7):
            total = total + got1[k, n].astype(F32)
        if k:
            send2[k] = total.astype(BF16)
            rs2.append(send(send2.at[k], got2.at[k], (rs2_s, rs2_r), (0, 0), at(4 * k, False)))
            rs2[-1].start()
        else:
            keep1[...] = total

    send(got_i.at[1:16], got_i.at[1:16], (rsi_s, rsi_r), (0, 0), {"user": twin}).wait_recv()
    total = part_i[u].astype(F32)
    for k in range(1, 16):
        total = total + got_i[k].astype(F32)
    item_out[...] = total.T * scale_i

    send(got2.at[1:4], got2.at[1:4], (rs2_s, rs2_r), (0, 0), at(1, False)).wait_recv()
    total = keep1[...]
    for k in range(1, 4):
        total = total + got2[k].astype(F32)
    user_out[...] = total * scale_u

    for c in ag_a + ag_i:
        c.wait_send()
    send(item_src.at[0:8], item_src.at[0:8], (ag_f_s, ag_f_r), (0, 0), {"user": twin}).wait_send()
    send(users.at[:, 0:7], users.at[:, 0:7], (ag_b_s, ag_b_r), (0, 0), at(1, False)).wait_send()
    send(part_u.at[:, 0:7], part_u.at[:, 0:7], (rs1_s, rs1_r), (0, 0), at(1, False)).wait_send()
    send(got_i.at[1:16], got_i.at[1:16], (rsi_s, rsi_r), (0, 0), {"user": twin}).wait_send()
    send(got2.at[1:4], got2.at[1:4], (rs2_s, rs2_r), (0, 0), at(1, False)).wait_send()


def hand_over(a, b, c, d, sem):
    copies = [pltpu.make_async_copy(a, c, sem.at[0]), pltpu.make_async_copy(b, d, sem.at[1])]
    for copy in copies:
        copy.start()
    for copy in copies:
        copy.wait()


def local(user_emb, item_emb, user_deg, item_deg, tile_rows, tile_cols, tile_count, tiles):
    hbm = pl.BlockSpec(memory_space=pltpu.HBM)
    dma = pltpu.SemaphoreType.DMA
    outs = (jax.ShapeDtypeStruct((SHARD, BLOCK), F32), jax.ShapeDtypeStruct((BLOCK, BLOCK), F32))
    vmem = pl.BlockSpec(memory_space=pltpu.VMEM)
    sums = pl.pallas_call(
        layer,
        out_shape=(pltpu.VMEM((SHARD, BLOCK), F32), pltpu.VMEM((BLOCK, BLOCK), F32)),
        in_specs=[hbm] * 8,
        out_specs=(vmem, vmem),
        scratch_shapes=[
            pltpu.VMEM((SHARD, BLOCK), F32),
            pltpu.VMEM((BLOCK, BLOCK), F32),
            pltpu.VMEM((UBLOCKS, BLOCK), I32),
            pltpu.VMEM((IBLOCKS, BLOCK), I32),
            pltpu.VMEM((1, 1, SLOTS), I32),
            pltpu.VMEM((1, 1, SLOTS), I32),
            pltpu.VMEM((1, 1), I32),
            pltpu.VMEM((SLOTS + 1, BLOCK, BLOCK), BF16),
            pltpu.VMEM((IBLOCKS, BLOCK, BLOCK), BF16),
            pltpu.VMEM((4, 8, SHARD, BLOCK), BF16),
            pltpu.VMEM((UBLOCKS, BLOCK, BLOCK), BF16),
            pltpu.VMEM((16, LANES), I32),
            pltpu.SMEM((16, LANES), I32),
            pltpu.VMEM((UPAIRS, BLOCK, BLOCK), F32),
            pltpu.VMEM((IPAIRS, BLOCK, BLOCK), F32),
            pltpu.VMEM((4, 8, SHARD, BLOCK), BF16),
            pltpu.VMEM((IBLOCKS, BLOCK, BLOCK), BF16),
            pltpu.VMEM((4, 7, SHARD, BLOCK), BF16),
            pltpu.VMEM((SHARD, BLOCK), F32),
            pltpu.VMEM((4, SHARD, BLOCK), BF16),
            pltpu.VMEM((4, SHARD, BLOCK), BF16),
            pltpu.VMEM((16, BLOCK, BLOCK), BF16),
            dma((11,)),
            dma((4,)), dma((4,)),
            dma((1,)), dma((1,)),
            dma((8,)), dma((8,)),
            dma((1,)), dma((1,)),
            dma((1,)), dma((4,)),
            dma((1,)), dma((1,)),
            dma((1,)), dma((1,)),
        ],
        compiler_params=pltpu.CompilerParams(
            collective_id=0, has_side_effects=True, vmem_limit_bytes=60 * 1024 * 1024
        ),
        name="layer",
    )(
        user_emb, item_emb, user_deg.reshape(UBLOCKS, BLOCK), item_deg.reshape(IBLOCKS, BLOCK),
        tile_rows, tile_cols, tile_count, tiles,
    )
    return pl.pallas_call(
        hand_over,
        out_shape=outs,
        in_specs=[vmem, vmem],
        out_specs=(hbm, hbm),
        scratch_shapes=[dma((2,))],
        compiler_params=pltpu.CompilerParams(vmem_limit_bytes=16 * 1024 * 1024),
        name="hand_over",
    )(*sums)


def solution(mesh):
    return jax.shard_map(
        local,
        mesh=mesh,
        in_specs=(
            P(("user", "item"), None),
            P(("item", "user"), None),
            P("user"),
            P("item"),
            P("user", "item", None),
            P("user", "item", None),
            P("user", "item"),
            P("user", "item", None, None, None),
        ),
        out_specs=(P(("user", "item"), None), P(("item", "user"), None)),
        check_vma=False,
    )
```

```python
import functools

import jax
import jax.numpy as jnp
from jax import lax
from jax.experimental import pallas as pl
from jax.experimental.pallas import tpu as pltpu
from jax.sharding import PartitionSpec as P

MESH = pl.DeviceIdType.MESH
F32, BF16, I32 = jnp.float32, jnp.bfloat16, jnp.int32

USERS_AXIS = 16
BLOCK = 128
SLOTS = 128
UBLOCKS, IBLOCKS = 12, 16
SHARD = 48
UPAIRS = (SLOTS + UBLOCKS) // 2
IPAIRS = (SLOTS + IBLOCKS) // 2
LANES = 256
UUNROLL, IUNROLL = 70, 72


def iota(shape, dim):
    return lax.broadcasted_iota(I32, shape, dim)


def count(mask, dim):
    return jnp.sum(jnp.where(mask, 1, 0).astype(I32), axis=dim, keepdims=True)


def column(lanes):
    eye = iota((SLOTS, SLOTS), 0) == iota((SLOTS, SLOTS), 1)
    return jnp.sum(jnp.where(eye, lanes, 0), axis=1, keepdims=True)


def order(keys, others, live):
    keys_c, others_c = column(keys), column(others)
    at_lane, at_row = iota((SLOTS, SLOTS), 1), iota((SLOTS, SLOTS), 0)
    alive_l = at_lane < live
    alive_c = iota((SLOTS, 1), 0) < live
    ahead = (keys_c == keys) & (at_lane < at_row) & alive_l
    rank_c = count(ahead, 1)
    hits_l = count((keys_c == at_lane) & (at_row < live), 0)
    hits_c = column(hits_l)
    padded_l = ((hits_l + 1) >> 1) << 1
    padded_c = ((hits_c + 1) >> 1) << 1
    base_l = jnp.sum(jnp.where(at_row < at_lane, padded_c, 0), axis=0, keepdims=True)
    base_c = jnp.sum(jnp.where(at_lane < at_row, padded_l, 0), axis=1, keepdims=True)
    place_c = jnp.sum(jnp.where(at_lane < keys_c, padded_l, 0), axis=1, keepdims=True) + rank_c
    places = iota((SLOTS, LANES), 1)
    slots = iota((SLOTS, LANES), 0)
    mine = (place_c == places) & alive_c
    slot = jnp.sum(jnp.where(mine, slots + 1, 0), axis=0, keepdims=True)
    slot = jnp.where(slot == 0, SLOTS, slot - 1)
    other = jnp.sum(jnp.where(mine, others_c, 0), axis=0, keepdims=True)
    opens = (base_c == places) & (hits_c > 0)
    keep = 1 - jnp.minimum(count(opens, 0), 1)
    last = ((base_l + padded_l) >> 1) - 1
    last = jnp.maximum(last, 0)
    some = jnp.minimum(hits_l, 1)
    return slot, other, keep, last, some


def own_scale(deg_ref, first, rows):
    blocks = deg_ref.shape[0]
    out = jnp.zeros((rows, 1), I32)
    for b in range(blocks):
        here = iota((rows, BLOCK), 1) + b * BLOCK == iota((rows, BLOCK), 0) + first
        out = out + jnp.sum(jnp.where(here, deg_ref[b : b + 1, :], 0), axis=1, keepdims=True)
    return lax.rsqrt(out.astype(F32))


def layer(
    user_emb_h, item_emb_h, user_deg_h, item_deg_h, rows_h, cols_h, live_h, tiles_h,
    user_out, item_out,
    user_emb, item_emb, user_deg, item_deg, rows_v, cols_v, live_v,
    tiles, item_src, users, user_src_t, meta_v, meta, run_u, run_i, part_u, part_i,
    got1, keep1, send2, got2, got_i,
    local_sem, ag_a_s, ag_a_r, ag_b_s, ag_b_r, ag_i_s, ag_i_r, ag_f_s, ag_f_r,
    rs1_s, rs1_r, rs2_s, rs2_r, rsi_s, rsi_r,
):
    u, i = lax.axis_index("user"), lax.axis_index("item")
    z, xh = i // 2, lax.rem(i, 2)
    zh, zl = z // 4, lax.rem(z, 4)
    kind = 2 * zl + xh
    twin = u + 1 - 2 * lax.rem(u, 2)

    def plane(dz):
        return lax.rem(z + dz + 16, 16)

    def at(dz, other):
        return {"item": 2 * plane(dz) + (1 - xh if other else xh)}

    def send(src, dst, sems, where, there):
        return pltpu.make_async_remote_copy(
            src_ref=src, dst_ref=dst, send_sem=sems[0].at[where[0]], recv_sem=sems[1].at[where[1]],
            device_id=there, device_id_type=MESH)

    ins = [
        pltpu.make_async_copy(a, b, local_sem.at[n]) for n, (a, b) in enumerate((
            (item_deg_h, item_deg), (item_emb_h, item_emb), (user_deg_h, user_deg), (user_emb_h, user_emb),
            (rows_h, rows_v), (cols_h, cols_v), (live_h, live_v), (tiles_h.at[0, 0], tiles.at[pl.ds(0, SLOTS)])))
    ]
    for c in ins:
        c.start()

    barrier = pltpu.get_barrier_semaphore()
    near = [(dz, o) for dz in (-2, -1, 0, 1, 2) for o in (False, True) if dz or o]
    far = [(8, False), (4, False), (12, False)]
    for dz, o in far + near:
        pl.semaphore_signal(barrier, inc=1, device_id=at(dz, o), device_id_type=MESH)
    for k in range(1, 8):
        pl.semaphore_signal(barrier, inc=1, device_id={"user": lax.rem(u + 2 * k, 16)}, device_id_type=MESH)
    pl.semaphore_signal(barrier, inc=1, device_id={"user": twin}, device_id_type=MESH)
    for k in range(1, 8):
        pl.semaphore_signal(barrier, inc=1, device_id={"user": lax.rem(twin + 2 * k, 16)}, device_id_type=MESH)

    for n in range(4):
        ins[n].wait()
    scale_i = own_scale(item_deg, u * BLOCK, BLOCK)
    item_src[u] = (item_emb[...] * scale_i).astype(BF16)
    scale_u = own_scale(user_deg, i * SHARD, SHARD)
    users[zh, kind] = (user_emb[...] * scale_u).astype(BF16)
    pl.semaphore_wait(barrier, 15 + len(near) + len(far))

    ag_a = [
        send(users.at[zh, kind], users.at[zh, kind], (ag_a_s, ag_a_r), (k, k), at(4 * k, False)) for k in (2, 1, 3)
    ]
    for c in ag_a:
        c.start()
    ag_i = [
        send(item_src.at[u], item_src.at[u], (ag_i_s, ag_i_r), (k, k), {"user": lax.rem(u + 2 * k, 16)})
        for k in range(1, 8)
    ]
    for c in ag_i:
        c.start()
    ag_f = [send(item_src.at[u], item_src.at[u], (ag_f_s, ag_f_r), (0, 0), {"user": twin})]
    ag_f[0].start()

    turn = 2 * plane(2) * (1 - xh) + 2 * plane(-2) * xh
    ag_b = []

    def spread(h):
        row = users.at[h, kind]
        for dz, o in ((0, True), (1, False), (1, True), (-1, False), (-1, True)):
            ag_b.append(send(row, row, (ag_b_s, ag_b_r), (0, 0), at(dz, o)))
        for half in range(2):
            ag_b.append(send(row, row, (ag_b_s, ag_b_r), (0, 0), {"item": turn + half}))
        for c in ag_b[-7:]:
            c.start()


    for n in range(4, 7):
        ins[n].wait()
    rows, cols, live = rows_v[0], cols_v[0], live_v[...]
    parts = order(rows, cols, live) + order(cols, rows, live)
    meta_v[...] = jnp.zeros_like(meta_v)
    for n, part in enumerate(parts):
        meta_v[n : n + 1, 0 : part.shape[1]] = part
    to_scalar = pltpu.make_async_copy(meta_v, meta, local_sem.at[8])
    to_scalar.start()
    tiles[SLOTS] = jnp.zeros((BLOCK, BLOCK), BF16)

    spread(zh)

    for k in range(1, 8):
        ag_i[k - 1].wait_recv()
        came = lax.rem(u - 2 * k + 16, 16)
        c = send(item_src.at[came], item_src.at[came], (ag_f_s, ag_f_r), (0, 0), {"user": twin})
        c.start()
        ag_f.append(c)
        if k in (4, 6):
            n = k // 2 - 1
            ag_a[n].wait_recv()
            spread(lax.rem(zh + (2 * n + 1), 4))
    ag_a[0].wait_recv()
    spread(lax.rem(zh + 2, 4))

    to_scalar.wait()
    ins[7].wait()
    send(item_src.at[0:8], item_src.at[0:8], (ag_f_s, ag_f_r), (0, 0), {"user": twin}).wait_recv()

    def user_step(q, acc):
        s0, s1 = meta[0, 2 * q], meta[0, 2 * q + 1]
        c0, c1 = meta[1, 2 * q], meta[1, 2 * q + 1]
        keep = meta[2, 2 * q].astype(F32)
        left = jnp.concatenate([tiles[s0], tiles[s1]], axis=1)
        right = jnp.concatenate([item_src[c0], item_src[c1]], axis=0)
        acc = acc * keep + jnp.dot(left, right, preferred_element_type=F32)
        run_u[q] = acc
        return acc

    lax.fori_loop(0, UPAIRS, user_step, jnp.zeros((BLOCK, BLOCK), F32), unroll=UUNROLL)
    for r in range(UBLOCKS):
        total = (run_u[meta[3, r]] * meta[4, r].astype(F32)).astype(BF16)
        for j in range(8):
            g = 8 * r + j
            part_u[g // 24, (g % 24) // 3, 16 * (g % 3) : 16 * (g % 3) + 16, :] = total[16 * j : 16 * j + 16]

    rs1 = []
    for k in (2, 1, 3, 0):
        for n, (dz, o) in enumerate(((0, True), (1, False), (1, True), (-1, False), (-1, True))):
            there = 2 * lax.rem(zl + dz + 4, 4) + (1 - xh if o else xh)
            rs1.append(send(part_u.at[lax.rem(plane(dz) // 4 + k, 4), there], got1.at[k, n], (rs1_s, rs1_r), (0, k), at(dz, o)))
        for half in range(2):
            there = 2 * lax.rem(zl + 2, 4) + half
            dz = 2 - 4 * half
            rs1.append(send(part_u.at[lax.rem(plane(dz) // 4 + k, 4), there], got1.at[k, 5 + xh], (rs1_s, rs1_r), (0, k),
                            {"item": 2 * plane(dz) + half}))
        for c in rs1[-7:]:
            c.start()

    send(users.at[:, 0:7], users.at[:, 0:7], (ag_b_s, ag_b_r), (0, 0), at(1, False)).wait_recv()
    for r in range(UBLOCKS):
        groups = []
        for j in range(8):
            g = 8 * r + j
            groups.append(users[g // 24, (g % 24) // 3, 16 * (g % 3) : 16 * (g % 3) + 16, :])
        user_src_t[r] = jnp.concatenate(groups, axis=0).T

    def item_step(q, acc):
        s0, s1 = meta[5, 2 * q], meta[5, 2 * q + 1]
        r0, r1 = meta[6, 2 * q], meta[6, 2 * q + 1]
        keep = meta[7, 2 * q].astype(F32)
        left = jnp.concatenate([user_src_t[r0], user_src_t[r1]], axis=1)
        right = jnp.concatenate([tiles[s0], tiles[s1]], axis=0)
        acc = acc * keep + jnp.dot(left, right, preferred_element_type=F32)
        run_i[q] = acc
        return acc

    lax.fori_loop(0, IPAIRS, item_step, jnp.zeros((BLOCK, BLOCK), F32), unroll=IUNROLL)
    for c in range(IBLOCKS):
        part_i[c] = (run_i[meta[8, c]] * meta[9, c].astype(F32)).astype(BF16)
    rsi = []
    for k in (12, 13, 4, 5, 11, 10, 14, 15, 6, 7, 3, 2, 9, 8, 1):
        there = lax.rem(u + k, 16)
        rsi.append(send(part_i.at[there], got_i.at[k], (rsi_s, rsi_r), (0, 0), {"user": there}))
    for c in rsi:
        c.start()

    rs2 = []
    for k in (2, 1, 3, 0):
        send(got1.at[k], got1.at[k], (rs1_s, rs1_r), (0, k), at(1, False)).wait_recv()
        total = part_u[lax.rem(zh + k, 4), kind].astype(F32)
        for n in range(7):
            total = total + got1[k, n].astype(F32)
        if k:
            send2[k] = total.astype(BF16)
            rs2.append(send(send2.at[k], got2.at[k], (rs2_s, rs2_r), (0, 0), at(4 * k, False)))
            rs2[-1].start()
        else:
            keep1[...] = total

    send(got_i.at[1:16], got_i.at[1:16], (rsi_s, rsi_r), (0, 0), {"user": twin}).wait_recv()
    total = part_i[u].astype(F32)
    for k in range(1, 16):
        total = total + got_i[k].astype(F32)
    item_out[...] = total.T * scale_i

    send(got2.at[1:4], got2.at[1:4], (rs2_s, rs2_r), (0, 0), at(1, False)).wait_recv()
    total = keep1[...]
    for k in range(1, 4):
        total = total + got2[k].astype(F32)
    user_out[...] = total * scale_u

    for c in ag_a + ag_i:
        c.wait_send()
    send(item_src.at[0:8], item_src.at[0:8], (ag_f_s, ag_f_r), (0, 0), {"user": twin}).wait_send()
    send(users.at[:, 0:7], users.at[:, 0:7], (ag_b_s, ag_b_r), (0, 0), at(1, False)).wait_send()
    send(part_u.at[:, 0:7], part_u.at[:, 0:7], (rs1_s, rs1_r), (0, 0), at(1, False)).wait_send()
    send(got_i.at[1:16], got_i.at[1:16], (rsi_s, rsi_r), (0, 0), {"user": twin}).wait_send()
    send(got2.at[1:4], got2.at[1:4], (rs2_s, rs2_r), (0, 0), at(1, False)).wait_send()


def hand_over(a, b, c, d, sem):
    copies = [pltpu.make_async_copy(a, c, sem.at[0]), pltpu.make_async_copy(b, d, sem.at[1])]
    for copy in copies:
        copy.start()
    for copy in copies:
        copy.wait()


def local(user_emb, item_emb, user_deg, item_deg, tile_rows, tile_cols, tile_count, tiles):
    hbm = pl.BlockSpec(memory_space=pltpu.HBM)
    dma = pltpu.SemaphoreType.DMA
    outs = (jax.ShapeDtypeStruct((SHARD, BLOCK), F32), jax.ShapeDtypeStruct((BLOCK, BLOCK), F32))
    vmem = pl.BlockSpec(memory_space=pltpu.VMEM)
    sums = pl.pallas_call(
        layer,
        out_shape=(pltpu.VMEM((SHARD, BLOCK), F32), pltpu.VMEM((BLOCK, BLOCK), F32)),
        in_specs=[hbm] * 8,
        out_specs=(vmem, vmem),
        scratch_shapes=[
            pltpu.VMEM((SHARD, BLOCK), F32),
            pltpu.VMEM((BLOCK, BLOCK), F32),
            pltpu.VMEM((UBLOCKS, BLOCK), I32),
            pltpu.VMEM((IBLOCKS, BLOCK), I32),
            pltpu.VMEM((1, 1, SLOTS), I32),
            pltpu.VMEM((1, 1, SLOTS), I32),
            pltpu.VMEM((1, 1), I32),
            pltpu.VMEM((SLOTS + 1, BLOCK, BLOCK), BF16),
            pltpu.VMEM((IBLOCKS, BLOCK, BLOCK), BF16),
            pltpu.VMEM((4, 8, SHARD, BLOCK), BF16),
            pltpu.VMEM((UBLOCKS, BLOCK, BLOCK), BF16),
            pltpu.VMEM((16, LANES), I32),
            pltpu.SMEM((16, LANES), I32),
            pltpu.VMEM((UPAIRS, BLOCK, BLOCK), F32),
            pltpu.VMEM((IPAIRS, BLOCK, BLOCK), F32),
            pltpu.VMEM((4, 8, SHARD, BLOCK), BF16),
            pltpu.VMEM((IBLOCKS, BLOCK, BLOCK), BF16),
            pltpu.VMEM((4, 7, SHARD, BLOCK), BF16),
            pltpu.VMEM((SHARD, BLOCK), F32),
            pltpu.VMEM((4, SHARD, BLOCK), BF16),
            pltpu.VMEM((4, SHARD, BLOCK), BF16),
            pltpu.VMEM((16, BLOCK, BLOCK), BF16),
            dma((11,)),
            dma((4,)), dma((4,)),
            dma((1,)), dma((1,)),
            dma((8,)), dma((8,)),
            dma((1,)), dma((1,)),
            dma((1,)), dma((4,)),
            dma((1,)), dma((1,)),
            dma((1,)), dma((1,)),
        ],
        compiler_params=pltpu.CompilerParams(
            collective_id=0, has_side_effects=True, vmem_limit_bytes=60 * 1024 * 1024
        ),
        name="layer",
    )(
        user_emb, item_emb, user_deg.reshape(UBLOCKS, BLOCK), item_deg.reshape(IBLOCKS, BLOCK),
        tile_rows, tile_cols, tile_count, tiles,
    )
    return pl.pallas_call(
        hand_over,
        out_shape=outs,
        in_specs=[vmem, vmem],
        out_specs=(hbm, hbm),
        scratch_shapes=[dma((2,))],
        compiler_params=pltpu.CompilerParams(vmem_limit_bytes=16 * 1024 * 1024),
        name="hand_over",
    )(*sums)


def solution(mesh):
    return jax.shard_map(
        local,
        mesh=mesh,
        in_specs=(
            P(("user", "item"), None),
            P(("item", "user"), None),
            P("user"),
            P("item"),
            P("user", "item", None),
            P("user", "item", None),
            P("user", "item"),
            P("user", "item", None, None, None),
        ),
        out_specs=(P(("user", "item"), None), P(("item", "user"), None)),
        check_vma=False,
    )
```
